512 devices in a mesh: row: 16 (over x, y), col: 16 (over z_lo, core), fiber: 2 (over z_hi).
Axes of the slice: x: 4, y: 4, z: 16 (z_hi: 2, z_lo: 8; z = z_hi * 8 + z_lo), core: 2. Of those that a mesh axis runs over, the one named last changes fastest.
Arguments:
- a_blocks: bfloat16 [64, 7, 128, 128], P(('row', 'fiber')), may hold values from -0.1875 to 0.1875
- p_terms: bfloat16 [64, 7, 128, 128], P(('row', 'fiber')), may hold values from -0.1875 to 0.1875
- block_columns: int32 [64, 7], replicated, may hold values from 0 to 63, as said below
- aggregates: int32 [64], replicated, may hold values from 0 to 15
Outputs:
- coarse: float32 [2048, 2048], P('row', 'col')
The draws below stay inside these ranges and needn't reach their ends.
Inputs may be any that keep to these rules, and one draw needn't show every extreme that they name: `block_columns`: each row names 7 distinct block columns, its own block row among them.
All inputs are finite; a program needn't handle non-finite values.
Results may differ from the reference program's by a relative error of at most 0.0003.
Values may be sent and summed in bfloat16 or wider, within the bound.
No kernel may reach another device: no remote copies, remote signals or barrier semaphores. Data moves between devices by JAX's collectives and lax.ppermute only.
A program may use at most 64 MiB of HBM per device.

```python
import jax
import jax.numpy as jnp
from jax import lax

BLK = 128
KA = 7
NFB = 64
NCB = 16


def draw_block_columns(key, part):
    key = jax.random.fold_in(key, 11)
    scores = jax.random.randint(key, (NFB, NFB), 0, 2 ** 20)
    order = jnp.arange(NFB, dtype=jnp.int32)
    scores = scores * NFB + order[None, :]
    scores = jnp.where(order[:, None] == order[None, :], 2 ** 30, scores)
    return lax.top_k(scores, KA)[1].astype(jnp.int32)


def touch_ends(result, stream_key, smallest, largest):
    extent = result.shape
    index_at = [jax.random.randint(jax.random.fold_in(stream_key, axis), (), 0, extent[axis]) for axis in range(len(extent))]
    result = result.at[tuple(index_at)].set(smallest)
    longest = extent.index(max(extent))
    index_at[longest] = (index_at[longest] + 1) % extent[longest]
    return result.at[tuple(index_at)].set(largest)


def shard_levels(key, shape, cuts, low, high):
    loudness = 1.0
    for axis_at, parts in cuts:
        heights = jax.random.uniform(jax.random.fold_in(jax.random.fold_in(key, 6), axis_at), (parts,), jnp.float32, low / len(cuts), high / len(cuts))
        loudness = loudness * jnp.repeat(jnp.exp(heights), shape[axis_at] // parts).reshape((-1,) + (1,) * (len(shape) - 1 - axis_at))
    return loudness


def scatter_about(own_key, shape, deviation, bound, cuts=(), kind=jnp.bfloat16):
    entries = jax.random.normal(own_key, shape, jnp.float32) * deviation
    if len(cuts) > 0:
        entries = shard_levels(own_key, shape, cuts, -0.22, 0.18) * entries
    return jnp.clip(entries, min=-bound, max=bound).astype(kind)


def setup_inputs(seed: int = 0) -> dict:
    keys = jax.random.split(jax.random.key(seed), 5)
    a_blocks = scatter_about(keys[0], (NFB, KA, BLK, BLK), (KA * BLK) ** -0.5, 0.1875, ((0, 32),))
    p_terms = scatter_about(keys[1], (NFB, KA, BLK, BLK), (KA * BLK) ** -0.5, 0.1875, ((0, 32),))
    block_columns = draw_block_columns(jax.random.fold_in(keys[4], 71), 0)
    aggregates = touch_ends(jax.random.randint(keys[3], (NFB,), 0, NCB), jax.random.fold_in(keys[3], 1), 0, NCB - 1).astype(jnp.int32)
    return {"a_blocks": a_blocks, "p_terms": p_terms, "block_columns": block_columns, "aggregates": aggregates}


def reference(a_blocks, p_terms, block_columns, aggregates):
    fine_total = block_columns.shape[0]
    fine_ids = jnp.arange(fine_total, dtype=jnp.int32)
    coarse_ids = jnp.arange(NCB, dtype=jnp.int32)
    hits = block_columns[:, :, None] == fine_ids[None, None, :]
    groups = jnp.sum(jnp.where(hits, aggregates[None, None, :], 0), axis=2).astype(jnp.int32)
    onehot = (groups[:, :, None] == coarse_ids[None, None, :]).astype(jnp.float32)
    terms_wide = p_terms.astype(jnp.float32)
    p_dense = jnp.einsum('ika,ikxy->ixay', onehot, terms_wide, precision=lax.Precision.HIGHEST)
    a_wide = a_blocks.astype(jnp.float32)

    def one_row(carry, inputs):
        a_row, cols, t_row, o_row = inputs
        neighbours = jnp.take(p_dense, cols.astype(jnp.int32), axis=0)
        y_row = jnp.einsum('kxz,kzay->xay', a_row, neighbours, precision=lax.Precision.HIGHEST)
        lifted = jnp.einsum('kxc,xay->kcay', t_row, y_row, precision=lax.Precision.HIGHEST)
        carry = carry + jnp.einsum('kb,kcay->bcay', o_row, lifted, precision=lax.Precision.HIGHEST)
        return carry, None

    start = jnp.zeros((NCB, BLK, NCB, BLK), jnp.float32)
    total, unused = lax.scan(one_row, start, (a_wide, block_columns, terms_wide, onehot))
    return total.reshape(NCB * BLK, NCB * BLK)
```

```python
import jax
import jax.numpy as jnp
from jax import lax
from jax.experimental import pallas as pl
from jax.experimental.pallas import tpu as pltpu
from jax.sharding import PartitionSpec as P

BLK = 128
HALF = 64
SCALE_ROWS = 16
TOP = 32766.0
STEPS = 64.0
F32 = jnp.float32
BF16 = jnp.bfloat16


def code(value):
    largest = jnp.max(jnp.abs(value), axis=0, keepdims=True)
    exponent = jnp.ceil(jnp.log2(jnp.maximum(largest, 2.0**-111)) * STEPS)
    steps = jnp.floor(value * (jnp.exp2(exponent * (-1.0 / STEPS)) * TOP) + 0.5)
    scale = jnp.broadcast_to(exponent, (SCALE_ROWS, value.shape[1]))
    return steps.astype(jnp.int32).astype(jnp.int16), scale.astype(jnp.int32).astype(jnp.int16)


def scale_of(codes):
    exponent = codes.astype(jnp.int32).astype(F32)[0:1]
    return jnp.exp2(exponent * (1.0 / STEPS)) * (1.0 / TOP)


def low_lanes(rows):
    return lax.broadcasted_iota(jnp.int32, (rows, BLK), 1) < HALF


def swap_halves(value):
    return pltpu.roll(value, HALF, 1)


def build_kernel(columns_ref, aggregates_ref, terms_ref, own_ref, partner_ref):
    rows, slots = terms_ref.shape[0], terms_ref.shape[1]
    nfiber = lax.axis_size("fiber")
    ncol = lax.axis_size("col")
    col = lax.axis_index("col")
    start = (lax.axis_index("row") * nfiber + lax.axis_index("fiber")) * rows
    working = lax.rem(col + ncol // 2, ncol)
    low = low_lanes(BLK)
    sums = [[], []]
    for q in range(rows):
        first = jnp.zeros((BLK, BLK), F32)
        second = jnp.zeros((BLK, BLK), F32)
        for k in range(slots):
            group = aggregates_ref[columns_ref[start + q, k]]
            term = terms_ref[q, k].astype(F32)
            first = first + term * jnp.where(group == working, 1.0, 0.0)
            second = second + term * jnp.where(group == col, 1.0, 0.0)
        sums[0].append(first)
        sums[1].append(second)
    for out_ref, (p0, p1) in zip((own_ref, partner_ref), sums):
        packed = (jnp.where(low, p0, swap_halves(p1)), jnp.where(low, swap_halves(p0), p1))
        for h in range(2):
            steps, scale = code(packed[h])
            out_ref[h, 0:BLK, :] = steps
            out_ref[h, BLK : BLK + SCALE_ROWS, :] = scale


def main_kernel(columns_ref, aggregates_ref, gathered_ref, a_own, p_own, a_pair, p_pair, out_ref, total):
    rows, slots = a_own.shape[0], a_own.shape[1]
    nfiber = lax.axis_size("fiber")
    fiber = lax.axis_index("fiber")
    row = lax.axis_index("row")
    low = low_lanes(BLK)
    lane_half = lax.broadcasted_iota(jnp.int32, (1, BLK), 1) // HALF
    total[...] = jnp.zeros_like(total)
    for a_ref, p_ref, panel in ((a_own, p_own, row), (a_pair, p_pair, row ^ 4)):
        for q in range(rows):
            i = (panel * nfiber + fiber) * rows + q
            y = jnp.zeros((BLK, 2 * BLK), F32)
            for k in range(slots):
                j = columns_ref[i, k]
                source = j // 4
                layer = (j // 2) % 2
                other = jnp.where(layer == fiber, 0, 1)
                factor = scale_of(gathered_ref[source, other, BLK : BLK + SCALE_ROWS, :])
                factor = jnp.where(lane_half == j % 2, factor, 0.0)
                block = gathered_ref[source, other, 0:BLK, :].astype(jnp.int32).astype(F32) * factor
                high = block.astype(BF16)
                rest = (block - high.astype(F32)).astype(BF16)
                y = y + jnp.dot(a_ref[q, k], jnp.concatenate([high, rest], axis=1), preferred_element_type=F32)
            y = y[:, :BLK] + y[:, BLK:]
            y = y + swap_halves(y)
            high = y.astype(BF16).astype(F32)
            split = jnp.where(low, high, y - high).astype(BF16)
            for k in range(slots):
                group = aggregates_ref[columns_ref[i, k]]
                lifted = lax.dot_general(p_ref[q, k], split, (((0,), (0,)), ((), ())), preferred_element_type=F32)
                total[group] += lifted
    low = low_lanes(HALF)
    for coarse in range(total.shape[0]):
        tile = total[coarse]
        tile = tile + swap_halves(tile)
        steps, scale = code(jnp.where(low, tile[:HALF], tile[HALF:]))
        out_ref[coarse, 0:HALF, :] = steps
        out_ref[coarse, HALF : HALF + SCALE_ROWS, :] = scale


def sum_kernel(parts_ref, out_ref):
    low = low_lanes(HALF)
    halves = [jnp.zeros((HALF, BLK), F32), jnp.zeros((HALF, BLK), F32)]
    for source in range(parts_ref.shape[0]):
        h = (source // 4) % 2
        factor = scale_of(parts_ref[source, HALF : HALF + SCALE_ROWS, :])
        halves[h] = halves[h] + parts_ref[source, 0:HALF, :].astype(jnp.int32).astype(F32) * factor
    left, right = halves
    out_ref[0:HALF, :] = jnp.where(low, left, swap_halves(right))
    out_ref[HALF:BLK, :] = jnp.where(low, swap_halves(left), right)


SMEM = pl.BlockSpec(memory_space=pltpu.SMEM)
VMEM = pl.BlockSpec(memory_space=pltpu.VMEM)


def local(a_blocks, p_terms, block_columns, aggregates):
    nrow = lax.axis_size("row")
    ncol = lax.axis_size("col")
    nfiber = lax.axis_size("fiber")
    pairs = [(r, r ^ 4) for r in range(nrow)]

    def along(step):
        moves = []
        for c in range(ncol):
            for f in range(nfiber):
                z = (f * (ncol // 2) + c // 2 + step) % ncol
                moves.append((c * nfiber + f, (z % (ncol // 2) * 2 + c % 2) * nfiber + z // (ncol // 2)))
        return moves

    across = [
        (c * nfiber + f, (c + ncol // 2) % ncol * nfiber + 1 - f) for c in range(ncol) for f in range(nfiber)
    ]
    unit = jax.ShapeDtypeStruct((2, BLK + SCALE_ROWS, BLK), jnp.int16)
    own, partner = pl.pallas_call(
        build_kernel,
        out_shape=(unit, unit),
        in_specs=[SMEM, SMEM, VMEM],
        out_specs=(VMEM, VMEM),
        name="build",
    )(block_columns, aggregates, p_terms)
    crossed = lax.ppermute(partner, ("col", "fiber"), across)
    a_pair = lax.ppermute(a_blocks, "row", pairs)
    p_pair = lax.ppermute(p_terms, "row", pairs)
    both = jnp.stack([own, crossed], axis=1)
    sent = jnp.broadcast_to(both[None, :, None], (nrow // 8, 2, 4) + both.shape[1:]).reshape((nrow,) + both.shape[1:])
    gathered = lax.all_to_all(sent, "row", 0, 0, tiled=True)
    parts = pl.pallas_call(
        main_kernel,
        out_shape=jax.ShapeDtypeStruct((nrow, HALF + SCALE_ROWS, BLK), jnp.int16),
        in_specs=[SMEM, SMEM] + [VMEM] * 5,
        out_specs=VMEM,
        scratch_shapes=[pltpu.VMEM((nrow, BLK, BLK), F32)],
        compiler_params=pltpu.CompilerParams(vmem_limit_bytes=32 * 1024 * 1024),
        name="main",
    )(block_columns, aggregates, gathered, a_blocks, p_terms, a_pair, p_pair)
    received = lax.all_to_all(parts, "row", 0, 0, tiled=True)
    tile = pl.pallas_call(
        sum_kernel,
        out_shape=jax.ShapeDtypeStruct((BLK, BLK), F32),
        in_specs=[VMEM],
        out_specs=VMEM,
        name="sum",
    )(received)
    up = lax.ppermute(tile, ("col", "fiber"), along(ncol // 4))
    down = lax.ppermute(tile, ("col", "fiber"), along(-(ncol // 4)))
    return up + down


def solution(mesh):
    in_specs = (
        P(("row", "fiber"), None, None, None),
        P(("row", "fiber"), None, None, None),
        P(),
        P(),
    )
    out_specs = P("row", "col")
    return jax.shard_map(local, mesh=mesh, in_specs=in_specs, out_specs=out_specs, check_vma=False)
```

```python
import jax
import jax.numpy as jnp
from jax import lax
from jax.experimental import pallas as pl
from jax.experimental.pallas import tpu as pltpu
from jax.sharding import PartitionSpec as P

BLK = 128
HALF = 64
SCALE_ROWS = 16
TOP = 32766.0
STEPS = 64.0
F32 = jnp.float32
BF16 = jnp.bfloat16


def code(value):
    largest = jnp.max(jnp.abs(value), axis=0, keepdims=True)
    exponent = jnp.ceil(jnp.log2(jnp.maximum(largest, 2.0**-111)) * STEPS)
    steps = jnp.floor(value * (jnp.exp2(exponent * (-1.0 / STEPS)) * TOP) + 0.5)
    scale = jnp.broadcast_to(exponent, (SCALE_ROWS, value.shape[1]))
    return steps.astype(jnp.int32).astype(jnp.int16), scale.astype(jnp.int32).astype(jnp.int16)


def scale_of(codes):
    exponent = codes[0:1].astype(F32)
    return jnp.exp2(exponent * (1.0 / STEPS)) * (1.0 / TOP)


def low_lanes(rows):
    return lax.broadcasted_iota(jnp.int32, (rows, BLK), 1) < HALF


def swap_halves(value):
    return pltpu.roll(value, HALF, 1)


def build_kernel(columns_ref, aggregates_ref, terms_ref, own_ref, partner_ref):
    rows, slots = terms_ref.shape[0], terms_ref.shape[1]
    nfiber = lax.axis_size("fiber")
    ncol = lax.axis_size("col")
    col = lax.axis_index("col")
    start = (lax.axis_index("row") * nfiber + lax.axis_index("fiber")) * rows
    working = lax.rem(col + ncol // 2, ncol)
    low = low_lanes(BLK)
    sums = [[], []]
    for q in range(rows):
        first = jnp.zeros((BLK, BLK), F32)
        second = jnp.zeros((BLK, BLK), F32)
        for k in range(slots):
            group = aggregates_ref[columns_ref[k, start + q]]
            term = terms_ref[q, k].astype(F32)
            first = first + term * jnp.where(group == working, 1.0, 0.0)
            second = second + term * jnp.where(group == col, 1.0, 0.0)
        sums[0].append(first)
        sums[1].append(second)
    for out_ref, (p0, p1) in zip((own_ref, partner_ref), sums):
        packed = (jnp.where(low, p0, swap_halves(p1)), jnp.where(low, swap_halves(p0), p1))
        for h in range(2):
            steps, scale = code(packed[h])
            targets = [r for r in range(own_ref.shape[0]) if r // 4 % 2 == h] if out_ref is own_ref else [h]
            for target in targets:
                out_ref[target, 0:BLK, :] = steps
                out_ref[target, BLK : BLK + SCALE_ROWS, :] = scale


def main_kernel(columns_ref, aggregates_ref, near_ref, far_ref, a_own, p_own, a_or_p, p_or_a, out_ref, total):
    rows, slots = a_own.shape[0], a_own.shape[1]
    nfiber = lax.axis_size("fiber")
    fiber = lax.axis_index("fiber")
    row = lax.axis_index("row")
    low = low_lanes(BLK)
    lane_half = lax.broadcasted_iota(jnp.int32, (1, BLK), 1) // HALF
    total[...] = jnp.zeros_like(total)
    first_core = lax.axis_index("col") % 2 == 0
    for a_ref, p_ref, panel in ((a_own, p_own, row), (a_or_p, p_or_a, row ^ 4)):
        paired = a_ref is a_or_p

        def blocks(ref, second_core_ref, q, k):
            if not paired:
                return ref[q, k]
            return jnp.where(first_core, ref[q, k], second_core_ref[q, k])

        for q in range(rows):
            i = (panel * nfiber + fiber) * rows + q
            y = jnp.zeros((BLK, 2 * BLK), F32)
            for k in range(slots):
                j = columns_ref[k, i]
                source = j // 4
                layer = (j // 2) % 2
                near = layer == fiber
                block, codes = [
                    jnp.where(near, near_ref[source, part].astype(jnp.int32), far_ref[source, part].astype(jnp.int32))
                    for part in (slice(0, BLK), slice(BLK, BLK + SCALE_ROWS))
                ]
                factor = jnp.where(lane_half == j % 2, scale_of(codes), 0.0)
                block = block.astype(F32) * factor
                high = block.astype(BF16)
                rest = (block - high.astype(F32)).astype(BF16)
                y = y + jnp.dot(blocks(a_ref, p_ref, q, k), jnp.concatenate([high, rest], axis=1), preferred_element_type=F32)
            y = y[:, :BLK] + y[:, BLK:]
            y = y + swap_halves(y)
            high = y.astype(BF16).astype(F32)
            split = jnp.where(low, high, y - high).astype(BF16)
            for k in range(slots):
                group = aggregates_ref[columns_ref[k, i]]
                lifted = lax.dot_general(blocks(p_ref, a_ref, q, k), split, (((0,), (0,)), ((), ())), preferred_element_type=F32)
                total[group] += lifted
    low = low_lanes(HALF)
    for coarse in range(total.shape[0]):
        tile = total[coarse]
        tile = tile + swap_halves(tile)
        steps, scale = code(jnp.where(low, tile[:HALF], tile[HALF:]))
        out_ref[coarse, 0:HALF, :] = steps
        out_ref[coarse, HALF : HALF + SCALE_ROWS, :] = scale


def sum_kernel(parts_ref, out_ref):
    low = low_lanes(HALF)
    halves = [jnp.zeros((HALF, BLK), F32), jnp.zeros((HALF, BLK), F32)]
    for source in range(parts_ref.shape[0]):
        h = (source // 4) % 2
        factor = scale_of(parts_ref[source, HALF : HALF + SCALE_ROWS, :].astype(jnp.int32))
        halves[h] = halves[h] + parts_ref[source, 0:HALF, :].astype(jnp.int32).astype(F32) * factor
    left, right = halves
    out_ref[0:HALF, :] = jnp.where(low, left, swap_halves(right))
    out_ref[HALF:BLK, :] = jnp.where(low, swap_halves(left), right)


SMEM = pl.BlockSpec(memory_space=pltpu.SMEM)
VMEM = pl.BlockSpec(memory_space=pltpu.VMEM)


def local(a_blocks, p_terms, block_columns, aggregates):
    nrow = lax.axis_size("row")
    ncol = lax.axis_size("col")
    nfiber = lax.axis_size("fiber")
    pairs = [(r, r ^ 4) for r in range(nrow)]

    def along(step):
        moves = []
        for c in range(ncol):
            for f in range(nfiber):
                z = (f * (ncol // 2) + c // 2 + step) % ncol
                moves.append((c * nfiber + f, (z % (ncol // 2) * 2 + c % 2) * nfiber + z // (ncol // 2)))
        return moves

    across = [
        (c * nfiber + f, (c + ncol // 2) % ncol * nfiber + 1 - f) for c in range(ncol) for f in range(nfiber)
    ]
    columns = block_columns.T
    packed_rows = BLK + SCALE_ROWS
    here = jnp.where(lax.axis_index("col") % 2 == 0, a_blocks, p_terms)
    from_pair = lax.ppermute(here, "row", pairs)
    own, partner = pl.pallas_call(
        build_kernel,
        out_shape=(
            jax.ShapeDtypeStruct((nrow, packed_rows, BLK), jnp.int16),
            jax.ShapeDtypeStruct((2, packed_rows, BLK), jnp.int16),
        ),
        in_specs=[SMEM, SMEM, VMEM],
        out_specs=(VMEM, VMEM),
        name="build",
    )(columns, aggregates, p_terms)
    crossed = lax.ppermute(partner, ("col", "fiber"), across)
    near = lax.all_to_all(own, "row", 0, 0, tiled=True)
    crossed = jnp.broadcast_to(crossed[None, :, None], (nrow // 8, 2, 4, packed_rows, BLK))
    far = lax.all_to_all(crossed.reshape(nrow, packed_rows, BLK), "row", 0, 0, tiled=True)
    from_core = lax.ppermute(from_pair, "col", [(c, c ^ 1) for c in range(ncol)])
    parts = pl.pallas_call(
        main_kernel,
        out_shape=jax.ShapeDtypeStruct((nrow, HALF + SCALE_ROWS, BLK), jnp.int16),
        in_specs=[SMEM, SMEM] + [VMEM] * 6,
        out_specs=VMEM,
        scratch_shapes=[pltpu.VMEM((nrow, BLK, BLK), F32)],
        compiler_params=pltpu.CompilerParams(vmem_limit_bytes=32 * 1024 * 1024),
        name="main",
    )(columns, aggregates, near, far, a_blocks, p_terms, from_pair, from_core)
    received = lax.all_to_all(parts, "row", 0, 0, tiled=True)
    tile = pl.pallas_call(
        sum_kernel,
        out_shape=jax.ShapeDtypeStruct((BLK, BLK), F32),
        in_specs=[VMEM],
        out_specs=VMEM,
        name="sum",
    )(received)
    up = lax.ppermute(tile, ("col", "fiber"), along(ncol // 4))
    down = lax.ppermute(tile, ("col", "fiber"), along(-(ncol // 4)))
    return up + down


def solution(mesh):
    in_specs = (
        P(("row", "fiber"), None, None, None),
        P(("row", "fiber"), None, None, None),
        P(),
        P(),
    )
    out_specs = P("row", "col")
    return jax.shard_map(local, mesh=mesh, in_specs=in_specs, out_specs=out_specs, check_vma=False)
```

```python
import jax
import jax.numpy as jnp
from jax import lax
from jax.experimental import pallas as pl
from jax.experimental.pallas import tpu as pltpu
from jax.sharding import PartitionSpec as P

BLK = 128
HALF = 64
SCALE_ROWS = 16
TOP = 32766.0
STEPS = 64.0
F32 = jnp.float32
BF16 = jnp.bfloat16


def code(value):
    largest = jnp.max(jnp.abs(value), axis=0, keepdims=True)
    exponent = jnp.ceil(jnp.log2(jnp.maximum(largest, 2.0**-111)) * STEPS)
    steps = jnp.floor(value * (jnp.exp2(exponent * (-1.0 / STEPS)) * TOP) + 0.5)
    scale = jnp.broadcast_to(exponent, (SCALE_ROWS, value.shape[1]))
    return steps.astype(jnp.int32).astype(jnp.int16), scale.astype(jnp.int32).astype(jnp.int16)


def scale_of(codes):
    exponent = codes[0:1].astype(F32)
    return jnp.exp2(exponent * (1.0 / STEPS)) * (1.0 / TOP)


def low_lanes(rows):
    return lax.broadcasted_iota(jnp.int32, (rows, BLK), 1) < HALF


def swap_halves(value):
    return pltpu.roll(value, HALF, 1)


def build_kernel(columns_ref, aggregates_ref, terms_ref, partner_ref, own_ref):
    rows, slots = terms_ref.shape[0], terms_ref.shape[1]
    ncol = lax.axis_size("col")
    col = lax.axis_index("col")
    start = (lax.axis_index("row") * lax.axis_size("fiber") + lax.axis_index("fiber")) * rows
    low = low_lanes(BLK)
    wanted = (col, lax.rem(col + ncol // 2, ncol))
    sums = [[], []]
    for q in range(rows):
        totals = [jnp.zeros((BLK, BLK), F32) for column in wanted]
        for k in range(slots):
            group = aggregates_ref[columns_ref[k, start + q]]
            term = terms_ref[q, k].astype(F32)
            totals = [t + term * jnp.where(group == column, 1.0, 0.0) for t, column in zip(totals, wanted)]
        for side, total in zip(sums, totals):
            side.append(total)
    for out_ref, (p0, p1) in zip((partner_ref, own_ref), sums):
        packed = (jnp.where(low, p0, swap_halves(p1)), jnp.where(low, swap_halves(p0), p1))
        for h in range(2):
            steps, scale = code(packed[h])
            for target in range(out_ref.shape[0]):
                if out_ref is partner_ref and target == h or out_ref is own_ref and target // 4 % 2 == h:
                    out_ref[target, 0:BLK, :] = steps
                    out_ref[target, BLK : BLK + SCALE_ROWS, :] = scale


def spread_kernel(pair_ref, out_ref):
    for target in range(out_ref.shape[0]):
        out_ref[target] = pair_ref[target // 4 % 2]


def main_kernel(columns_ref, aggregates_ref, near_ref, far_ref, a_own, p_own, a_or_p, p_or_a, out_ref, total):
    rows, slots = a_own.shape[0], a_own.shape[1]
    nfiber = lax.axis_size("fiber")
    fiber = lax.axis_index("fiber")
    row = lax.axis_index("row")
    low = low_lanes(BLK)
    lane_half = lax.broadcasted_iota(jnp.int32, (1, BLK), 1) // HALF
    total[...] = jnp.zeros_like(total)
    first_core = lax.axis_index("col") % 2 == 0
    for a_ref, p_ref, panel in ((a_own, p_own, row), (a_or_p, p_or_a, row ^ 4)):
        paired = a_ref is a_or_p

        def blocks(ref, second_core_ref, q, k):
            if not paired:
                return ref[q, k]
            return jnp.where(first_core, ref[q, k], second_core_ref[q, k])

        for q in range(rows):
            i = (panel * nfiber + fiber) * rows + q
            y = jnp.zeros((BLK, 2 * BLK), F32)
            for k in range(slots):
                j = columns_ref[k, i]
                source = j // 4
                layer = (j // 2) % 2
                near = layer == fiber
                block, codes = [
                    jnp.where(near, near_ref[source, part].astype(jnp.int32), far_ref[source, part].astype(jnp.int32))
                    for part in (slice(0, BLK), slice(BLK, BLK + SCALE_ROWS))
                ]
                factor = jnp.where(lane_half == j % 2, scale_of(codes), 0.0)
                block = block.astype(F32) * factor
                high = block.astype(BF16)
                rest = (block - high.astype(F32)).astype(BF16)
                y = y + jnp.dot(blocks(a_ref, p_ref, q, k), jnp.concatenate([high, rest], axis=1), preferred_element_type=F32)
            y = y[:, :BLK] + y[:, BLK:]
            y = y + swap_halves(y)
            high = y.astype(BF16).astype(F32)
            split = jnp.where(low, high, y - high).astype(BF16)
            for k in range(slots):
                group = aggregates_ref[columns_ref[k, i]]
                lifted = lax.dot_general(blocks(p_ref, a_ref, q, k), split, (((0,), (0,)), ((), ())), preferred_element_type=F32)
                total[group] += lifted
    low = low_lanes(HALF)
    for coarse in range(total.shape[0]):
        tile = total[coarse]
        tile = tile + swap_halves(tile)
        steps, scale = code(jnp.where(low, tile[:HALF], tile[HALF:]))
        out_ref[coarse, 0:HALF, :] = steps
        out_ref[coarse, HALF : HALF + SCALE_ROWS, :] = scale


def sum_kernel(parts_ref, out_ref):
    low = low_lanes(HALF)
    halves = [jnp.zeros((HALF, BLK), F32), jnp.zeros((HALF, BLK), F32)]
    for source in range(parts_ref.shape[0]):
        h = (source // 4) % 2
        factor = scale_of(parts_ref[source, HALF : HALF + SCALE_ROWS, :].astype(jnp.int32))
        halves[h] = halves[h] + parts_ref[source, 0:HALF, :].astype(jnp.int32).astype(F32) * factor
    left, right = halves
    out_ref[0:HALF, :] = jnp.where(low, left, swap_halves(right))
    out_ref[HALF:BLK, :] = jnp.where(low, swap_halves(left), right)


SMEM = pl.BlockSpec(memory_space=pltpu.SMEM)
VMEM = pl.BlockSpec(memory_space=pltpu.VMEM)


def local(a_blocks, p_terms, block_columns, aggregates):
    nrow = lax.axis_size("row")
    ncol = lax.axis_size("col")
    nfiber = lax.axis_size("fiber")
    pairs = [(r, r ^ 4) for r in range(nrow)]

    def along(step):
        moves = []
        for c in range(ncol):
            for f in range(nfiber):
                z = (f * (ncol // 2) + c // 2 + step) % ncol
                moves.append((c * nfiber + f, (z % (ncol // 2) * 2 + c % 2) * nfiber + z // (ncol // 2)))
        return moves

    across = [
        (c * nfiber + f, (c + ncol // 2) % ncol * nfiber + 1 - f) for c in range(ncol) for f in range(nfiber)
    ]
    columns = block_columns.T
    packed_rows = BLK + SCALE_ROWS
    partner, own = pl.pallas_call(
        build_kernel,
        out_shape=(
            jax.ShapeDtypeStruct((2, packed_rows, BLK), jnp.int16),
            jax.ShapeDtypeStruct((nrow, packed_rows, BLK), jnp.int16),
        ),
        in_specs=[SMEM, SMEM, VMEM],
        out_specs=(VMEM, VMEM),
        name="build",
    )(columns, aggregates, p_terms)
    here = jnp.where(lax.axis_index("col") % 2 == 0, a_blocks, p_terms)
    from_pair = lax.ppermute(here, "row", pairs)
    crossed = lax.ppermute(partner, ("col", "fiber"), across)
    near = lax.all_to_all(own, "row", 0, 0, tiled=True)
    spread = pl.pallas_call(
        spread_kernel,
        out_shape=jax.ShapeDtypeStruct((nrow, packed_rows, BLK), jnp.int16),
        in_specs=[VMEM],
        out_specs=VMEM,
        cost_estimate=pl.CostEstimate(flops=2**37, bytes_accessed=2**21, transcendentals=0),
        compiler_params=pltpu.CompilerParams(vmem_limit_bytes=4 * 1024 * 1024),
        name="spread",
    )(crossed)
    far = lax.all_to_all(spread, "row", 0, 0, tiled=True)
    from_core = lax.ppermute(from_pair, "col", [(c, c ^ 1) for c in range(ncol)])
    parts = pl.pallas_call(
        main_kernel,
        out_shape=jax.ShapeDtypeStruct((nrow, HALF + SCALE_ROWS, BLK), jnp.int16),
        in_specs=[SMEM, SMEM] + [VMEM] * 6,
        out_specs=VMEM,
        scratch_shapes=[pltpu.VMEM((nrow, BLK, BLK), F32)],
        compiler_params=pltpu.CompilerParams(vmem_limit_bytes=16 * 1024 * 1024),
        name="main",
    )(columns, aggregates, near, far, a_blocks, p_terms, from_pair, from_core)
    received = lax.all_to_all(parts, "row", 0, 0, tiled=True)
    tile = pl.pallas_call(
        sum_kernel,
        out_shape=jax.ShapeDtypeStruct((BLK, BLK), F32),
        in_specs=[VMEM],
        out_specs=VMEM,
        compiler_params=pltpu.CompilerParams(vmem_limit_bytes=4 * 1024 * 1024),
        name="sum",
    )(received)
    up = lax.ppermute(tile, ("col", "fiber"), along(ncol // 4))
    down = lax.ppermute(tile, ("col", "fiber"), along(-(ncol // 4)))
    return up + down


def solution(mesh):
    in_specs = (
        P(("row", "fiber"), None, None, None),
        P(("row", "fiber"), None, None, None),
        P(),
        P(),
    )
    out_specs = P("row", "col")
    return jax.shard_map(local, mesh=mesh, in_specs=in_specs, out_specs=out_specs, check_vma=False)
```

```python
import jax
import jax.numpy as jnp
from jax import lax
from jax.experimental import pallas as pl
from jax.experimental.pallas import tpu as pltpu
from jax.sharding import PartitionSpec as P

BLK = 128
HALF = 64
SCALE_ROWS = 16
TOP = 32766.0
STEPS = 64.0
F32 = jnp.float32
BF16 = jnp.bfloat16


def code(value):
    largest = jnp.max(jnp.abs(value), axis=0, keepdims=True)
    exponent = jnp.ceil(jnp.log2(jnp.maximum(largest, 2.0**-111)) * STEPS)
    steps = jnp.floor(value * (jnp.exp2(exponent * (-1.0 / STEPS)) * TOP) + 0.5)
    scale = jnp.broadcast_to(exponent, (SCALE_ROWS, value.shape[1]))
    return steps.astype(jnp.int32).astype(jnp.int16), scale.astype(jnp.int32).astype(jnp.int16)


def scale_of(codes):
    exponent = codes[0:1].astype(F32)
    return jnp.exp2(exponent * (1.0 / STEPS)) * (1.0 / TOP)


def low_lanes(rows):
    return lax.broadcasted_iota(jnp.int32, (rows, BLK), 1) < HALF


def swap_halves(value):
    return pltpu.roll(value, HALF, 1)


def build_kernel(columns_ref, aggregates_ref, terms_ref, partner_ref, own_ref):
    rows, slots = terms_ref.shape[0], terms_ref.shape[1]
    ncol = lax.axis_size("col")
    col = lax.axis_index("col")
    start = (lax.axis_index("row") * lax.axis_size("fiber") + lax.axis_index("fiber")) * rows
    low = low_lanes(BLK)
    wanted = (lax.rem(col + ncol // 2, ncol), col)
    sums = [[], []]
    for q in range(rows):
        totals = [jnp.zeros((BLK, BLK), F32) for column in wanted]
        for k in range(slots):
            group = aggregates_ref[columns_ref[k, start + q]]
            term = terms_ref[q, k].astype(F32)
            totals = [t + term * jnp.where(group == column, 1.0, 0.0) for t, column in zip(totals, wanted)]
        for side, total in zip(sums, totals):
            side.append(total)
    for out_ref, (p0, p1) in zip((partner_ref, own_ref), sums):
        packed = (jnp.where(low, p0, swap_halves(p1)), jnp.where(low, swap_halves(p0), p1))
        for h in range(2):
            steps, scale = code(packed[h])
            for target in range(out_ref.shape[0]):
                if out_ref is partner_ref and target == h or out_ref is own_ref and target // 4 % 2 == h:
                    out_ref[target, 0:BLK, :] = steps
                    out_ref[target, BLK : BLK + SCALE_ROWS, :] = scale


def spread_kernel(pair_ref, out_ref):
    for target in range(out_ref.shape[0]):
        out_ref[target] = pair_ref[target // 4 % 2]


def main_kernel(columns_ref, aggregates_ref, near_ref, far_ref, a_own, p_own, a_or_p, p_or_a, out_ref, total):
    rows, slots = a_own.shape[0], a_own.shape[1]
    nfiber = lax.axis_size("fiber")
    fiber = lax.axis_index("fiber")
    row = lax.axis_index("row")
    lane_half = lax.broadcasted_iota(jnp.int32, (1, BLK), 1) // HALF
    total[...] = jnp.zeros_like(total)
    first_core = lax.axis_index("col") % 2 == 0

    def own_row(ref, second_core_ref, q):
        return jnp.concatenate([ref[q, k] for k in range(slots)], axis=1)

    def pair_row(ref, second_core_ref, q):
        return jnp.concatenate([jnp.where(first_core, ref[q, k], second_core_ref[q, k]) for k in range(slots)], axis=1)

    for a_ref, p_ref, panel, blocks in ((a_own, p_own, row, own_row), (a_or_p, p_or_a, row ^ 4, pair_row)):
        for q in range(rows):
            i = (panel * nfiber + fiber) * rows + q
            neighbours = []
            for k in range(slots):
                j = columns_ref[k, i]
                source = j // 4
                near = (j // 2) % 2 == fiber
                block, codes = [
                    jnp.where(near, near_ref[source, part].astype(jnp.int32), far_ref[source, part].astype(jnp.int32))
                    for part in (slice(0, BLK), slice(BLK, BLK + SCALE_ROWS))
                ]
                factor = jnp.where(lane_half == j % 2, scale_of(codes), 0.0)
                block = block.astype(F32) * factor
                high = block.astype(BF16)
                rest = (block - high.astype(F32)).astype(BF16)
                neighbours.append(jnp.concatenate([high, rest], axis=1))
            y = jnp.dot(
                blocks(a_ref, p_ref, q), jnp.concatenate(neighbours, axis=0), preferred_element_type=F32
            )
            y = (y[:, :BLK] + y[:, BLK:]).T
            y = y[:HALF] + y[HALF:]
            high = y.astype(BF16)
            rest = (y - high.astype(F32)).astype(BF16)
            lifted = jnp.dot(
                jnp.concatenate([high, rest], axis=0), blocks(p_ref, a_ref, q), preferred_element_type=F32
            )
            lifted = lifted[:HALF] + lifted[HALF:]
            for k in range(slots):
                group = aggregates_ref[columns_ref[k, i]]
                total[group] += lifted[:, k * BLK : (k + 1) * BLK]
    for coarse in range(total.shape[0]):
        steps, scale = code(total[coarse])
        out_ref[coarse, 0:HALF, :] = steps
        out_ref[coarse, HALF : HALF + SCALE_ROWS, :] = scale


def sum_kernel(parts_ref, out_ref):
    halves = [jnp.zeros((HALF, BLK), F32), jnp.zeros((HALF, BLK), F32)]
    for source in range(parts_ref.shape[0]):
        h = (source // 4) % 2
        factor = scale_of(parts_ref[source, HALF : HALF + SCALE_ROWS, :].astype(jnp.int32))
        halves[h] = halves[h] + parts_ref[source, 0:HALF, :].astype(jnp.int32).astype(F32) * factor
    out_ref[...] = jnp.concatenate(halves, axis=0).T


SMEM = pl.BlockSpec(memory_space=pltpu.SMEM)
VMEM = pl.BlockSpec(memory_space=pltpu.VMEM)


def local(a_blocks, p_terms, block_columns, aggregates):
    nrow = lax.axis_size("row")
    ncol = lax.axis_size("col")
    nfiber = lax.axis_size("fiber")
    pairs = [(r, r ^ 4) for r in range(nrow)]

    def along(step):
        moves = []
        for c in range(ncol):
            for f in range(nfiber):
                z = (f * (ncol // 2) + c // 2 + step) % ncol
                moves.append((c * nfiber + f, (z % (ncol // 2) * 2 + c % 2) * nfiber + z // (ncol // 2)))
        return moves

    across = [
        (c * nfiber + f, (c + ncol // 2) % ncol * nfiber + 1 - f) for c in range(ncol) for f in range(nfiber)
    ]
    columns = block_columns.T
    packed_rows = BLK + SCALE_ROWS
    partner, own = pl.pallas_call(
        build_kernel,
        out_shape=(
            jax.ShapeDtypeStruct((2, packed_rows, BLK), jnp.int16),
            jax.ShapeDtypeStruct((nrow, packed_rows, BLK), jnp.int16),
        ),
        in_specs=[SMEM, SMEM, VMEM],
        out_specs=(VMEM, VMEM),
        name="build",
    )(columns, aggregates, p_terms)
    here = jnp.where(lax.axis_index("col") % 2 == 0, a_blocks, p_terms)
    from_pair = lax.ppermute(here, "row", pairs)
    crossed = lax.ppermute(partner, ("col", "fiber"), across)
    near = lax.all_to_all(own, "row", 0, 0, tiled=True)
    spread = pl.pallas_call(
        spread_kernel,
        out_shape=jax.ShapeDtypeStruct((nrow, packed_rows, BLK), jnp.int16),
        in_specs=[VMEM],
        out_specs=VMEM,
        cost_estimate=pl.CostEstimate(flops=2**37, bytes_accessed=2**21, transcendentals=0),
        compiler_params=pltpu.CompilerParams(vmem_limit_bytes=4 * 1024 * 1024),
        name="spread",
    )(crossed)
    far = lax.all_to_all(spread, "row", 0, 0, tiled=True)
    from_core = lax.ppermute(from_pair, "col", [(c, c ^ 1) for c in range(ncol)])
    parts = pl.pallas_call(
        main_kernel,
        out_shape=jax.ShapeDtypeStruct((nrow, HALF + SCALE_ROWS, BLK), jnp.int16),
        in_specs=[SMEM, SMEM] + [VMEM] * 6,
        out_specs=VMEM,
        scratch_shapes=[pltpu.VMEM((nrow, HALF, BLK), F32)],
        compiler_params=pltpu.CompilerParams(vmem_limit_bytes=16 * 1024 * 1024),
        name="main",
    )(columns, aggregates, near, far, a_blocks, p_terms, from_pair, from_core)
    received = lax.all_to_all(parts, "row", 0, 0, tiled=True)
    tile = pl.pallas_call(
        sum_kernel,
        out_shape=jax.ShapeDtypeStruct((BLK, BLK), F32),
        in_specs=[VMEM],
        out_specs=VMEM,
        compiler_params=pltpu.CompilerParams(vmem_limit_bytes=4 * 1024 * 1024),
        name="sum",
    )(received)
    layers = lax.all_gather(tile, "fiber")
    return layers[0] + layers[1]


def solution(mesh):
    in_specs = (
        P(("row", "fiber"), None, None, None),
        P(("row", "fiber"), None, None, None),
        P(),
        P(),
    )
    out_specs = P("row", "col")
    return jax.shard_map(local, mesh=mesh, in_specs=in_specs, out_specs=out_specs, check_vma=False)
```

```python
import jax
import jax.numpy as jnp
from jax import lax
from jax.experimental import pallas as pl
from jax.experimental.pallas import tpu as pltpu
from jax.sharding import PartitionSpec as P

BLK = 128
HALF = 64
SCALE_ROWS = 16
TOP = 32766.0
STEPS = 64.0
F32 = jnp.float32
BF16 = jnp.bfloat16


def code(value):
    largest = jnp.max(jnp.abs(value), axis=0, keepdims=True)
    exponent = jnp.ceil(jnp.log2(jnp.maximum(largest, 2.0**-111)) * STEPS)
    steps = jnp.floor(value * (jnp.exp2(exponent * (-1.0 / STEPS)) * TOP) + 0.5)
    scale = jnp.broadcast_to(exponent, (SCALE_ROWS // 2, value.shape[1]))
    return steps.astype(jnp.int32), scale.astype(jnp.int32)


def scale_of(codes):
    exponent = codes[0:1].astype(F32)
    return jnp.exp2(exponent * (1.0 / STEPS)) * (1.0 / TOP)


def build_kernel(columns_ref, aggregates_ref, terms_ref, partner_ref, own_ref):
    rows, slots = terms_ref.shape[0], terms_ref.shape[1]
    ncol = lax.axis_size("col")
    col = lax.axis_index("col")
    start = (lax.axis_index("row") * lax.axis_size("fiber") + lax.axis_index("fiber")) * rows
    wanted = (lax.rem(col + ncol // 2, ncol), col)
    sums = [[], []]
    for q in range(rows):
        totals = [jnp.zeros((BLK, BLK), F32) for column in wanted]
        for k in range(slots):
            group = aggregates_ref[columns_ref[k, start + q]]
            term = terms_ref[q, k].astype(F32)
            totals = [t + term * jnp.where(group == column, 1.0, 0.0) for t, column in zip(totals, wanted)]
        for side, total in zip(sums, totals):
            side.append(total)
    for out_ref, blocks in zip((partner_ref, own_ref), sums):
        blocks = [block.T for block in blocks]
        for h in range(2):
            steps, scales = zip(*[code(block[h * HALF : (h + 1) * HALF]) for block in blocks])
            steps, scales = jnp.concatenate(steps, axis=0), jnp.concatenate(scales, axis=0)
            for target in range(out_ref.shape[0]):
                if out_ref is partner_ref and target == h or out_ref is own_ref and target // 4 % 2 == h:
                    out_ref[target, 0:BLK, :] = steps.astype(jnp.int16)
                    out_ref[target, BLK : BLK + SCALE_ROWS, :] = scales.astype(jnp.int16)


def spread_kernel(pair_ref, out_ref):
    for target in range(out_ref.shape[0]):
        out_ref[target] = pair_ref[target // 4 % 2]


def main_kernel(columns_ref, aggregates_ref, near_ref, far_ref, a_own, p_own, a_or_p, p_or_a, out_ref, total):
    rows, slots = a_own.shape[0], a_own.shape[1]
    nfiber = lax.axis_size("fiber")
    fiber = lax.axis_index("fiber")
    row = lax.axis_index("row")
    total[...] = jnp.zeros_like(total)
    first_core = lax.axis_index("col") % 2 == 0

    def own_row(ref, second_core_ref, q):
        return jnp.concatenate([ref[q, k] for k in range(slots)], axis=1)

    def pair_row(ref, second_core_ref, q):
        return jnp.concatenate([jnp.where(first_core, ref[q, k], second_core_ref[q, k]) for k in range(slots)], axis=1)

    sides = ((a_own, p_own, row, own_row), (a_or_p, p_or_a, row ^ 4, pair_row))
    fine = [(*side, q, (side[2] * nfiber + fiber) * rows + q) for side in sides for q in range(rows)]
    products = []
    for a_ref, p_ref, panel, blocks, q, i in fine:
        neighbours = []
        for k in range(slots):
            j = columns_ref[k, i]
            source = j // 4
            near = (j // 2) % 2 == fiber
            place = pl.ds(pl.multiple_of(j % 2 * HALF, HALF), HALF)
            block, codes = [
                jnp.where(near, near_ref[source, part].astype(jnp.int32), far_ref[source, part].astype(jnp.int32))
                for part in (place, slice(BLK, BLK + SCALE_ROWS))
            ]
            codes = jnp.where(j % 2 == 0, codes[0:1], codes[SCALE_ROWS // 2 : SCALE_ROWS // 2 + 1])
            block = block.astype(F32) * scale_of(codes)
            high = block.astype(BF16)
            rest = (block - high.astype(F32)).astype(BF16)
            neighbours.append(jnp.concatenate([high, rest], axis=0))
        products.append(
            lax.dot_general(
                jnp.concatenate(neighbours, axis=1),
                blocks(a_ref, p_ref, q),
                (((1,), (1,)), ((), ())),
                preferred_element_type=F32,
            )
        )
    lifted = []
    for (a_ref, p_ref, panel, blocks, q, i), y in zip(fine, products):
        y = y[:HALF] + y[HALF:]
        high = y.astype(BF16)
        rest = (y - high.astype(F32)).astype(BF16)
        both = jnp.dot(jnp.concatenate([high, rest], axis=0), blocks(p_ref, a_ref, q), preferred_element_type=F32)
        lifted.append(both[:HALF] + both[HALF:])
    for (a_ref, p_ref, panel, blocks, q, i), part in zip(fine, lifted):
        for k in range(slots):
            group = aggregates_ref[columns_ref[k, i]]
            total[group] += part[:, k * BLK : (k + 1) * BLK]
    for coarse in range(total.shape[0]):
        steps, scale = code(total[coarse])
        out_ref[coarse, 0:HALF, :] = steps.astype(jnp.int16)
        out_ref[coarse, HALF : HALF + SCALE_ROWS, :] = jnp.concatenate([scale, scale], axis=0).astype(jnp.int16)


def sum_kernel(parts_ref, out_ref):
    halves = [jnp.zeros((HALF, BLK), F32), jnp.zeros((HALF, BLK), F32)]
    for source in range(parts_ref.shape[0]):
        h = (source // 4) % 2
        factor = scale_of(parts_ref[source, HALF : HALF + SCALE_ROWS, :].astype(jnp.int32))
        halves[h] = halves[h] + parts_ref[source, 0:HALF, :].astype(jnp.int32).astype(F32) * factor
    steps, scale = code(jnp.concatenate(halves, axis=0).T)
    out_ref[0:BLK, :] = steps.astype(jnp.int16)
    out_ref[BLK : BLK + SCALE_ROWS, :] = jnp.concatenate([scale, scale], axis=0).astype(jnp.int16)


def add_kernel(layers_ref, out_ref):
    total = jnp.zeros_like(out_ref)
    for layer in range(layers_ref.shape[0]):
        factor = scale_of(layers_ref[layer, BLK : BLK + SCALE_ROWS, :].astype(jnp.int32))
        total = total + layers_ref[layer, 0:BLK, :].astype(jnp.int32).astype(F32) * factor
    out_ref[...] = total


SMEM = pl.BlockSpec(memory_space=pltpu.SMEM)
VMEM = pl.BlockSpec(memory_space=pltpu.VMEM)


def local(a_blocks, p_terms, block_columns, aggregates):
    nrow = lax.axis_size("row")
    ncol = lax.axis_size("col")
    nfiber = lax.axis_size("fiber")
    pairs = [(r, r ^ 4) for r in range(nrow)]

    def along(step):
        moves = []
        for c in range(ncol):
            for f in range(nfiber):
                z = (f * (ncol // 2) + c // 2 + step) % ncol
                moves.append((c * nfiber + f, (z % (ncol // 2) * 2 + c % 2) * nfiber + z // (ncol // 2)))
        return moves

    across = [
        (c * nfiber + f, (c + ncol // 2) % ncol * nfiber + 1 - f) for c in range(ncol) for f in range(nfiber)
    ]
    columns = block_columns.T
    packed_rows = BLK + SCALE_ROWS
    partner, own = pl.pallas_call(
        build_kernel,
        out_shape=(
            jax.ShapeDtypeStruct((2, packed_rows, BLK), jnp.int16),
            jax.ShapeDtypeStruct((nrow, packed_rows, BLK), jnp.int16),
        ),
        in_specs=[SMEM, SMEM, VMEM],
        out_specs=(VMEM, VMEM),
        name="build",
    )(columns, aggregates, p_terms)
    here = jnp.where(lax.axis_index("col") % 2 == 0, a_blocks, p_terms)
    from_pair = lax.ppermute(here, "row", pairs)
    crossed = lax.ppermute(partner, ("col", "fiber"), across)
    near = lax.all_to_all(own, "row", 0, 0, tiled=True)
    spread = pl.pallas_call(
        spread_kernel,
        out_shape=jax.ShapeDtypeStruct((nrow, packed_rows, BLK), jnp.int16),
        in_specs=[VMEM],
        out_specs=VMEM,
        cost_estimate=pl.CostEstimate(flops=2**37, bytes_accessed=2**21, transcendentals=0),
        compiler_params=pltpu.CompilerParams(vmem_limit_bytes=4 * 1024 * 1024),
        name="spread",
    )(crossed)
    far = lax.all_to_all(spread, "row", 0, 0, tiled=True)
    from_core = lax.ppermute(from_pair, "col", [(c, c ^ 1) for c in range(ncol)])
    parts = pl.pallas_call(
        main_kernel,
        out_shape=jax.ShapeDtypeStruct((nrow, HALF + SCALE_ROWS, BLK), jnp.int16),
        in_specs=[SMEM, SMEM] + [VMEM] * 6,
        out_specs=VMEM,
        scratch_shapes=[pltpu.VMEM((nrow, HALF, BLK), F32)],
        compiler_params=pltpu.CompilerParams(vmem_limit_bytes=16 * 1024 * 1024),
        name="main",
    )(columns, aggregates, near, far, a_blocks, p_terms, from_pair, from_core)
    received = lax.all_to_all(parts, "row", 0, 0, tiled=True)
    tile = pl.pallas_call(
        sum_kernel,
        out_shape=jax.ShapeDtypeStruct((packed_rows, BLK), jnp.int16),
        in_specs=[VMEM],
        out_specs=VMEM,
        compiler_params=pltpu.CompilerParams(vmem_limit_bytes=4 * 1024 * 1024),
        name="sum",
    )(received)
    layers = lax.all_gather(tile, "fiber")
    return pl.pallas_call(
        add_kernel,
        out_shape=jax.ShapeDtypeStruct((BLK, BLK), F32),
        in_specs=[VMEM],
        out_specs=VMEM,
        compiler_params=pltpu.CompilerParams(vmem_limit_bytes=4 * 1024 * 1024),
        name="add",
    )(layers)


def solution(mesh):
    in_specs = (
        P(("row", "fiber"), None, None, None),
        P(("row", "fiber"), None, None, None),
        P(),
        P(),
    )
    out_specs = P("row", "col")
    return jax.shard_map(local, mesh=mesh, in_specs=in_specs, out_specs=out_specs, check_vma=False)
```

```python
import jax
import jax.numpy as jnp
from jax import lax
from jax.experimental import pallas as pl
from jax.experimental.pallas import tpu as pltpu
from jax.sharding import PartitionSpec as P

BLK = 128
HALF = 64
SCALE_ROWS = 16
TOP = 32766.0
STEPS = 64.0
F32 = jnp.float32
BF16 = jnp.bfloat16


ORDER = (0, 10)


def slot_of(row_index):
    return row_index ^ jnp.where(lax.axis_index("col") % 2 == 0, ORDER[0], ORDER[1])


def code(value):
    largest = jnp.max(jnp.abs(value), axis=0, keepdims=True)
    exponent = jnp.ceil(jnp.log2(jnp.maximum(largest, 2.0**-111)) * STEPS)
    steps = jnp.floor(value * (jnp.exp2(exponent * (-1.0 / STEPS)) * TOP) + 0.5)
    scale = jnp.broadcast_to(exponent, (SCALE_ROWS // 2, value.shape[1]))
    return steps.astype(jnp.int32), scale.astype(jnp.int32)


def scale_of(codes):
    exponent = codes[0:1].astype(F32)
    return jnp.exp2(exponent * (1.0 / STEPS)) * (1.0 / TOP)


def build_kernel(columns_ref, aggregates_ref, terms_ref, partner_ref, own_ref):
    rows, slots = terms_ref.shape[0], terms_ref.shape[1]
    ncol = lax.axis_size("col")
    col = lax.axis_index("col")
    start = (lax.axis_index("row") * lax.axis_size("fiber") + lax.axis_index("fiber")) * rows
    wanted = (lax.rem(col + ncol // 2, ncol), col)
    sums = [[], []]
    for q in range(rows):
        totals = [jnp.zeros((BLK, BLK), F32) for column in wanted]
        for k in range(slots):
            group = aggregates_ref[columns_ref[k, start + q]]
            term = terms_ref[q, k].astype(F32)
            totals = [t + term * jnp.where(group == column, 1.0, 0.0) for t, column in zip(totals, wanted)]
        for side, total in zip(sums, totals):
            side.append(total)
    for out_ref, blocks in zip((partner_ref, own_ref), sums):
        blocks = [block.T for block in blocks]
        for h in range(2):
            steps, scales = zip(*[code(block[h * HALF : (h + 1) * HALF]) for block in blocks])
            steps, scales = jnp.concatenate(steps, axis=0), jnp.concatenate(scales, axis=0)
            for target in range(out_ref.shape[0]):
                if out_ref is partner_ref and target == h or out_ref is own_ref and target // 4 % 2 == h:
                    slot = target if out_ref is partner_ref else slot_of(target)
                    out_ref[slot, 0:BLK, :] = steps.astype(jnp.int16)
                    out_ref[slot, BLK : BLK + SCALE_ROWS, :] = scales.astype(jnp.int16)


def spread_kernel(pair_ref, out_ref):
    for target in range(out_ref.shape[0]):
        out_ref[slot_of(target)] = pair_ref[target // 4 % 2]


def main_kernel(columns_ref, aggregates_ref, near_ref, far_ref, a_own, p_own, a_or_p, p_or_a, out_ref, total):
    rows, slots = a_own.shape[0], a_own.shape[1]
    nfiber = lax.axis_size("fiber")
    fiber = lax.axis_index("fiber")
    row = lax.axis_index("row")
    total[...] = jnp.zeros_like(total)
    first_core = lax.axis_index("col") % 2 == 0

    def own_row(ref, second_core_ref, q):
        return jnp.concatenate([ref[q, k] for k in range(slots)], axis=1)

    def pair_row(ref, second_core_ref, q):
        return jnp.concatenate([jnp.where(first_core, ref[q, k], second_core_ref[q, k]) for k in range(slots)], axis=1)

    sides = ((a_own, p_own, row, own_row), (a_or_p, p_or_a, row ^ 4, pair_row))
    fine = [(*side, q, (side[2] * nfiber + fiber) * rows + q) for side in sides for q in range(rows)]
    products = []
    for a_ref, p_ref, panel, blocks, q, i in fine:
        neighbours = []
        for k in range(slots):
            j = columns_ref[k, i]
            source = slot_of(j // 4)
            near = (j // 2) % 2 == fiber
            place = pl.ds(pl.multiple_of(j % 2 * HALF, HALF), HALF)
            block, codes = [
                jnp.where(near, near_ref[source, part].astype(jnp.int32), far_ref[source, part].astype(jnp.int32))
                for part in (place, slice(BLK, BLK + SCALE_ROWS))
            ]
            codes = jnp.where(j % 2 == 0, codes[0:1], codes[SCALE_ROWS // 2 : SCALE_ROWS // 2 + 1])
            block = block.astype(F32) * scale_of(codes)
            high = block.astype(BF16)
            rest = (block - high.astype(F32)).astype(BF16)
            neighbours.append(jnp.concatenate([high, rest], axis=0))
        products.append(
            lax.dot_general(
                jnp.concatenate(neighbours, axis=1),
                blocks(a_ref, p_ref, q),
                (((1,), (1,)), ((), ())),
                preferred_element_type=F32,
            )
        )
    lifted = []
    for (a_ref, p_ref, panel, blocks, q, i), y in zip(fine, products):
        y = y[:HALF] + y[HALF:]
        high = y.astype(BF16)
        rest = (y - high.astype(F32)).astype(BF16)
        both = jnp.dot(jnp.concatenate([high, rest], axis=0), blocks(p_ref, a_ref, q), preferred_element_type=F32)
        lifted.append(both[:HALF] + both[HALF:])
    for (a_ref, p_ref, panel, blocks, q, i), part in zip(fine, lifted):
        for k in range(slots):
            group = aggregates_ref[columns_ref[k, i]]
            total[group] += part[:, k * BLK : (k + 1) * BLK]
    for coarse in range(total.shape[0]):
        steps, scale = code(total[coarse])
        slot = slot_of(coarse)
        out_ref[slot, 0:HALF, :] = steps.astype(jnp.int16)
        out_ref[slot, HALF : HALF + SCALE_ROWS, :] = jnp.concatenate([scale, scale], axis=0).astype(jnp.int16)


def sum_kernel(parts_ref, out_ref):
    halves = [jnp.zeros((HALF, BLK), F32), jnp.zeros((HALF, BLK), F32)]
    for source in range(parts_ref.shape[0]):
        h = (source // 4) % 2
        slot = slot_of(source)
        factor = scale_of(parts_ref[slot, HALF : HALF + SCALE_ROWS, :].astype(jnp.int32))
        halves[h] = halves[h] + parts_ref[slot, 0:HALF, :].astype(jnp.int32).astype(F32) * factor
    steps, scale = code(jnp.concatenate(halves, axis=0).T)
    out_ref[0:BLK, :] = steps.astype(jnp.int16)
    out_ref[BLK : BLK + SCALE_ROWS, :] = jnp.concatenate([scale, scale], axis=0).astype(jnp.int16)


def add_kernel(layers_ref, out_ref):
    total = jnp.zeros_like(out_ref)
    for layer in range(layers_ref.shape[0]):
        factor = scale_of(layers_ref[layer, BLK : BLK + SCALE_ROWS, :].astype(jnp.int32))
        total = total + layers_ref[layer, 0:BLK, :].astype(jnp.int32).astype(F32) * factor
    out_ref[...] = total


SMEM = pl.BlockSpec(memory_space=pltpu.SMEM)
VMEM = pl.BlockSpec(memory_space=pltpu.VMEM)


def local(a_blocks, p_terms, block_columns, aggregates):
    nrow = lax.axis_size("row")
    ncol = lax.axis_size("col")
    nfiber = lax.axis_size("fiber")
    pairs = [(r, r ^ 4) for r in range(nrow)]

    def along(step):
        moves = []
        for c in range(ncol):
            for f in range(nfiber):
                z = (f * (ncol // 2) + c // 2 + step) % ncol
                moves.append((c * nfiber + f, (z % (ncol // 2) * 2 + c % 2) * nfiber + z // (ncol // 2)))
        return moves

    across = [
        (c * nfiber + f, (c + ncol // 2) % ncol * nfiber + 1 - f) for c in range(ncol) for f in range(nfiber)
    ]

    orders = [[(k ^ ORDER[c % 2]) * ncol + c for k in range(nrow)] for c in range(ncol)]
    columns = block_columns.T
    packed_rows = BLK + SCALE_ROWS
    partner, own = pl.pallas_call(
        build_kernel,
        out_shape=(
            jax.ShapeDtypeStruct((2, packed_rows, BLK), jnp.int16),
            jax.ShapeDtypeStruct((nrow, packed_rows, BLK), jnp.int16),
        ),
        in_specs=[SMEM, SMEM, VMEM],
        out_specs=(VMEM, VMEM),
        name="build",
    )(columns, aggregates, p_terms)
    here = jnp.where(lax.axis_index("col") % 2 == 0, a_blocks, p_terms)
    from_pair = lax.ppermute(here, "row", pairs)
    crossed = lax.ppermute(partner, ("col", "fiber"), across)
    near = lax.all_to_all(own, ("row", "col"), 0, 0, axis_index_groups=orders, tiled=True)
    spread = pl.pallas_call(
        spread_kernel,
        out_shape=jax.ShapeDtypeStruct((nrow, packed_rows, BLK), jnp.int16),
        in_specs=[VMEM],
        out_specs=VMEM,
        cost_estimate=pl.CostEstimate(flops=2**37, bytes_accessed=2**21, transcendentals=0),
        compiler_params=pltpu.CompilerParams(vmem_limit_bytes=4 * 1024 * 1024),
        name="spread",
    )(crossed)
    far = lax.all_to_all(spread, ("row", "col"), 0, 0, axis_index_groups=orders, tiled=True)
    from_core = lax.ppermute(from_pair, "col", [(c, c ^ 1) for c in range(ncol)])
    parts = pl.pallas_call(
        main_kernel,
        out_shape=jax.ShapeDtypeStruct((nrow, HALF + SCALE_ROWS, BLK), jnp.int16),
        in_specs=[SMEM, SMEM] + [VMEM] * 6,
        out_specs=VMEM,
        scratch_shapes=[pltpu.VMEM((nrow, HALF, BLK), F32)],
        compiler_params=pltpu.CompilerParams(vmem_limit_bytes=16 * 1024 * 1024),
        name="main",
    )(columns, aggregates, near, far, a_blocks, p_terms, from_pair, from_core)
    received = lax.all_to_all(parts, ("row", "col"), 0, 0, axis_index_groups=orders, tiled=True)
    tile = pl.pallas_call(
        sum_kernel,
        out_shape=jax.ShapeDtypeStruct((packed_rows, BLK), jnp.int16),
        in_specs=[VMEM],
        out_specs=VMEM,
        compiler_params=pltpu.CompilerParams(vmem_limit_bytes=4 * 1024 * 1024),
        name="sum",
    )(received)
    layers = lax.all_gather(tile, "fiber")
    return pl.pallas_call(
        add_kernel,
        out_shape=jax.ShapeDtypeStruct((BLK, BLK), F32),
        in_specs=[VMEM],
        out_specs=VMEM,
        compiler_params=pltpu.CompilerParams(vmem_limit_bytes=4 * 1024 * 1024),
        name="add",
    )(layers)


def solution(mesh):
    in_specs = (
        P(("row", "fiber"), None, None, None),
        P(("row", "fiber"), None, None, None),
        P(),
        P(),
    )
    out_specs = P("row", "col")
    return jax.shard_map(local, mesh=mesh, in_specs=in_specs, out_specs=out_specs, check_vma=False)
```

```python
import jax
import jax.numpy as jnp
from jax import lax
from jax.experimental import pallas as pl
from jax.experimental.pallas import tpu as pltpu
from jax.sharding import PartitionSpec as P

BLK = 128
HALF = 64
SCALE_ROWS = 16
TOP = 32766.0
STEPS = 64.0
F32 = jnp.float32
BF16 = jnp.bfloat16


NEAR = (0, 10)
LATER = (10, 5)


def slot_of(row_index, masks):
    return row_index ^ jnp.where(lax.axis_index("col") % 2 == 0, masks[0], masks[1])


def code(value):
    largest = jnp.max(jnp.abs(value), axis=0, keepdims=True)
    exponent = jnp.ceil(jnp.log2(jnp.maximum(largest, 2.0**-111)) * STEPS)
    steps = jnp.floor(value * (jnp.exp2(exponent * (-1.0 / STEPS)) * TOP) + 0.5)
    scale = jnp.broadcast_to(exponent, (SCALE_ROWS // 2, value.shape[1]))
    return steps.astype(jnp.int32), scale.astype(jnp.int32)


def scale_of(codes):
    exponent = codes[0:1].astype(F32)
    return jnp.exp2(exponent * (1.0 / STEPS)) * (1.0 / TOP)


def build_kernel(columns_ref, aggregates_ref, terms_ref, partner_ref, own_ref):
    rows, slots = terms_ref.shape[0], terms_ref.shape[1]
    ncol = lax.axis_size("col")
    col = lax.axis_index("col")
    start = (lax.axis_index("row") * lax.axis_size("fiber") + lax.axis_index("fiber")) * rows
    wanted = (lax.rem(col + ncol // 2, ncol), col)
    sums = [[], []]
    for q in range(rows):
        totals = [jnp.zeros((BLK, BLK), F32) for column in wanted]
        for k in range(slots):
            group = aggregates_ref[columns_ref[k, start + q]]
            term = terms_ref[q, k].astype(F32)
            totals = [t + term * jnp.where(group == column, 1.0, 0.0) for t, column in zip(totals, wanted)]
        for side, total in zip(sums, totals):
            side.append(total)
    for out_ref, blocks in zip((partner_ref, own_ref), sums):
        blocks = [block.T for block in blocks]
        for h in range(2):
            steps, scales = zip(*[code(block[h * HALF : (h + 1) * HALF]) for block in blocks])
            steps, scales = jnp.concatenate(steps, axis=0), jnp.concatenate(scales, axis=0)
            for target in range(out_ref.shape[0]):
                if out_ref is partner_ref and target == h or out_ref is own_ref and target // 4 % 2 == h:
                    slot = target if out_ref is partner_ref else slot_of(target, NEAR)
                    out_ref[slot, 0:BLK, :] = steps.astype(jnp.int16)
                    out_ref[slot, BLK : BLK + SCALE_ROWS, :] = scales.astype(jnp.int16)


def spread_kernel(pair_ref, out_ref):
    for target in range(out_ref.shape[0]):
        out_ref[slot_of(target, LATER)] = pair_ref[target // 4 % 2]


def main_kernel(columns_ref, aggregates_ref, near_ref, far_ref, a_own, p_own, a_or_p, p_or_a, out_ref, total):
    rows, slots = a_own.shape[0], a_own.shape[1]
    nfiber = lax.axis_size("fiber")
    fiber = lax.axis_index("fiber")
    row = lax.axis_index("row")
    total[...] = jnp.zeros_like(total)
    first_core = lax.axis_index("col") % 2 == 0

    def own_row(ref, second_core_ref, q):
        return jnp.concatenate([ref[q, k] for k in range(slots)], axis=1)

    def pair_row(ref, second_core_ref, q):
        return jnp.concatenate([jnp.where(first_core, ref[q, k], second_core_ref[q, k]) for k in range(slots)], axis=1)

    sides = ((a_own, p_own, row, own_row), (a_or_p, p_or_a, row ^ 4, pair_row))
    fine = [(*side, q, (side[2] * nfiber + fiber) * rows + q) for side in sides for q in range(rows)]
    products = []
    for a_ref, p_ref, panel, blocks, q, i in fine:
        neighbours = []
        for k in range(slots):
            j = columns_ref[k, i]
            near_slot, far_slot = slot_of(j // 4, NEAR), slot_of(j // 4, LATER)
            near = (j // 2) % 2 == fiber
            place = pl.ds(pl.multiple_of(j % 2 * HALF, HALF), HALF)
            block, codes = [
                jnp.where(near, near_ref[near_slot, part].astype(jnp.int32), far_ref[far_slot, part].astype(jnp.int32))
                for part in (place, slice(BLK, BLK + SCALE_ROWS))
            ]
            codes = jnp.where(j % 2 == 0, codes[0:1], codes[SCALE_ROWS // 2 : SCALE_ROWS // 2 + 1])
            block = block.astype(F32) * scale_of(codes)
            high = block.astype(BF16)
            rest = (block - high.astype(F32)).astype(BF16)
            neighbours.append(jnp.concatenate([high, rest], axis=0))
        products.append(
            lax.dot_general(
                jnp.concatenate(neighbours, axis=1),
                blocks(a_ref, p_ref, q),
                (((1,), (1,)), ((), ())),
                preferred_element_type=F32,
            )
        )
    lifted = []
    for (a_ref, p_ref, panel, blocks, q, i), y in zip(fine, products):
        y = y[:HALF] + y[HALF:]
        high = y.astype(BF16)
        rest = (y - high.astype(F32)).astype(BF16)
        both = jnp.dot(jnp.concatenate([high, rest], axis=0), blocks(p_ref, a_ref, q), preferred_element_type=F32)
        lifted.append(both[:HALF] + both[HALF:])
    for (a_ref, p_ref, panel, blocks, q, i), part in zip(fine, lifted):
        for k in range(slots):
            group = aggregates_ref[columns_ref[k, i]]
            total[group] += part[:, k * BLK : (k + 1) * BLK]
    for coarse in range(total.shape[0]):
        steps, scale = code(total[coarse])
        slot = slot_of(coarse, LATER)
        out_ref[slot, 0:HALF, :] = steps.astype(jnp.int16)
        out_ref[slot, HALF : HALF + SCALE_ROWS, :] = jnp.concatenate([scale, scale], axis=0).astype(jnp.int16)


def sum_kernel(parts_ref, out_ref):
    halves = [jnp.zeros((HALF, BLK), F32), jnp.zeros((HALF, BLK), F32)]
    for source in range(parts_ref.shape[0]):
        h = (source // 4) % 2
        slot = slot_of(source, LATER)
        factor = scale_of(parts_ref[slot, HALF : HALF + SCALE_ROWS, :].astype(jnp.int32))
        halves[h] = halves[h] + parts_ref[slot, 0:HALF, :].astype(jnp.int32).astype(F32) * factor
    steps, scale = code(jnp.concatenate(halves, axis=0).T)
    out_ref[0:BLK, :] = steps.astype(jnp.int16)
    out_ref[BLK : BLK + SCALE_ROWS, :] = jnp.concatenate([scale, scale], axis=0).astype(jnp.int16)


def add_kernel(layers_ref, out_ref):
    total = jnp.zeros_like(out_ref)
    for layer in range(layers_ref.shape[0]):
        factor = scale_of(layers_ref[layer, BLK : BLK + SCALE_ROWS, :].astype(jnp.int32))
        total = total + layers_ref[layer, 0:BLK, :].astype(jnp.int32).astype(F32) * factor
    out_ref[...] = total


SMEM = pl.BlockSpec(memory_space=pltpu.SMEM)
VMEM = pl.BlockSpec(memory_space=pltpu.VMEM)


def local(a_blocks, p_terms, block_columns, aggregates):
    nrow = lax.axis_size("row")
    ncol = lax.axis_size("col")
    nfiber = lax.axis_size("fiber")
    pairs = [(r, r ^ 4) for r in range(nrow)]

    def along(step):
        moves = []
        for c in range(ncol):
            for f in range(nfiber):
                z = (f * (ncol // 2) + c // 2 + step) % ncol
                moves.append((c * nfiber + f, (z % (ncol // 2) * 2 + c % 2) * nfiber + z // (ncol // 2)))
        return moves

    across = [
        (c * nfiber + f, (c + ncol // 2) % ncol * nfiber + 1 - f) for c in range(ncol) for f in range(nfiber)
    ]

    def orders(masks):
        return [[(k ^ masks[c % 2]) * ncol + c for k in range(nrow)] for c in range(ncol)]

    columns = block_columns.T
    packed_rows = BLK + SCALE_ROWS
    partner, own = pl.pallas_call(
        build_kernel,
        out_shape=(
            jax.ShapeDtypeStruct((2, packed_rows, BLK), jnp.int16),
            jax.ShapeDtypeStruct((nrow, packed_rows, BLK), jnp.int16),
        ),
        in_specs=[SMEM, SMEM, VMEM],
        out_specs=(VMEM, VMEM),
        name="build",
    )(columns, aggregates, p_terms)
    here = jnp.where(lax.axis_index("col") % 2 == 0, a_blocks, p_terms)
    from_pair = lax.ppermute(here, "row", pairs)
    crossed = lax.ppermute(partner, ("col", "fiber"), across)
    near = lax.all_to_all(own, ("row", "col"), 0, 0, axis_index_groups=orders(NEAR), tiled=True)
    spread = pl.pallas_call(
        spread_kernel,
        out_shape=jax.ShapeDtypeStruct((nrow, packed_rows, BLK), jnp.int16),
        in_specs=[VMEM],
        out_specs=VMEM,
        cost_estimate=pl.CostEstimate(flops=2**37, bytes_accessed=2**21, transcendentals=0),
        compiler_params=pltpu.CompilerParams(vmem_limit_bytes=4 * 1024 * 1024),
        name="spread",
    )(crossed)
    far = lax.all_to_all(spread, ("row", "col"), 0, 0, axis_index_groups=orders(LATER), tiled=True)
    from_core = lax.ppermute(from_pair, "col", [(c, c ^ 1) for c in range(ncol)])
    parts = pl.pallas_call(
        main_kernel,
        out_shape=jax.ShapeDtypeStruct((nrow, HALF + SCALE_ROWS, BLK), jnp.int16),
        in_specs=[SMEM, SMEM] + [VMEM] * 6,
        out_specs=VMEM,
        scratch_shapes=[pltpu.VMEM((nrow, HALF, BLK), F32)],
        compiler_params=pltpu.CompilerParams(vmem_limit_bytes=16 * 1024 * 1024),
        name="main",
    )(columns, aggregates, near, far, a_blocks, p_terms, from_pair, from_core)
    received = lax.all_to_all(parts, ("row", "col"), 0, 0, axis_index_groups=orders(LATER), tiled=True)
    tile = pl.pallas_call(
        sum_kernel,
        out_shape=jax.ShapeDtypeStruct((packed_rows, BLK), jnp.int16),
        in_specs=[VMEM],
        out_specs=VMEM,
        compiler_params=pltpu.CompilerParams(vmem_limit_bytes=4 * 1024 * 1024),
        name="sum",
    )(received)
    layers = lax.all_gather(tile, "fiber")
    return pl.pallas_call(
        add_kernel,
        out_shape=jax.ShapeDtypeStruct((BLK, BLK), F32),
        in_specs=[VMEM],
        out_specs=VMEM,
        compiler_params=pltpu.CompilerParams(vmem_limit_bytes=4 * 1024 * 1024),
        name="add",
    )(layers)


def solution(mesh):
    in_specs = (
        P(("row", "fiber"), None, None, None),
        P(("row", "fiber"), None, None, None),
        P(),
        P(),
    )
    out_specs = P("row", "col")
    return jax.shard_map(local, mesh=mesh, in_specs=in_specs, out_specs=out_specs, check_vma=False)
```

```python
import jax
import jax.numpy as jnp
from jax import lax
from jax.experimental import pallas as pl
from jax.experimental.pallas import tpu as pltpu
from jax.sharding import PartitionSpec as P

BLK = 128
HALF = 64
SCALE_ROWS = 16
TOP = 32766.0
STEPS = 64.0
F32 = jnp.float32
BF16 = jnp.bfloat16


NEAR = (0, 10)
LATER = (10, 5)


def turned(row_index):
    return row_index % 4 * 4 + row_index // 4


def later_slot(row_index):
    return jnp.where(lax.axis_index("col") % 2 == 0, turned(row_index ^ LATER[0]), turned(row_index ^ LATER[1]))


def slot_of(row_index, masks):
    return row_index ^ jnp.where(lax.axis_index("col") % 2 == 0, masks[0], masks[1])


def code(value):
    largest = jnp.max(jnp.abs(value), axis=0, keepdims=True)
    exponent = jnp.ceil(jnp.log2(jnp.maximum(largest, 2.0**-111)) * STEPS)
    steps = jnp.floor(value * (jnp.exp2(exponent * (-1.0 / STEPS)) * TOP) + 0.5)
    scale = jnp.broadcast_to(exponent, (SCALE_ROWS // 2, value.shape[1]))
    return steps.astype(jnp.int32), scale.astype(jnp.int32)


def scale_of(codes):
    exponent = codes[0:1].astype(F32)
    return jnp.exp2(exponent * (1.0 / STEPS)) * (1.0 / TOP)


def build_kernel(columns_ref, aggregates_ref, terms_ref, partner_ref, own_ref):
    rows, slots = terms_ref.shape[0], terms_ref.shape[1]
    ncol = lax.axis_size("col")
    col = lax.axis_index("col")
    start = (lax.axis_index("row") * lax.axis_size("fiber") + lax.axis_index("fiber")) * rows
    wanted = (lax.rem(col + ncol // 2, ncol), col)
    sums = [[], []]
    for q in range(rows):
        totals = [jnp.zeros((BLK, BLK), F32) for column in wanted]
        for k in range(slots):
            group = aggregates_ref[columns_ref[k, start + q]]
            term = terms_ref[q, k].astype(F32)
            totals = [t + term * jnp.where(group == column, 1.0, 0.0) for t, column in zip(totals, wanted)]
        for side, total in zip(sums, totals):
            side.append(total)
    for out_ref, blocks in zip((partner_ref, own_ref), sums):
        blocks = [block.T for block in blocks]
        for h in range(2):
            steps, scales = zip(*[code(block[h * HALF : (h + 1) * HALF]) for block in blocks])
            steps, scales = jnp.concatenate(steps, axis=0), jnp.concatenate(scales, axis=0)
            for target in range(out_ref.shape[0]):
                if out_ref is partner_ref and target == h or out_ref is own_ref and target // 4 % 2 == h:
                    slot = target if out_ref is partner_ref else slot_of(target, NEAR)
                    out_ref[slot, 0:BLK, :] = steps.astype(jnp.int16)
                    out_ref[slot, BLK : BLK + SCALE_ROWS, :] = scales.astype(jnp.int16)


def spread_kernel(pair_ref, out_ref):
    for target in range(out_ref.shape[0]):
        out_ref[later_slot(target)] = pair_ref[target // 4 % 2]


def main_kernel(columns_ref, aggregates_ref, near_ref, far_ref, a_own, p_own, a_or_p, p_or_a, out_ref, total):
    rows, slots = a_own.shape[0], a_own.shape[1]
    nfiber = lax.axis_size("fiber")
    fiber = lax.axis_index("fiber")
    row = lax.axis_index("row")
    total[...] = jnp.zeros_like(total)
    first_core = lax.axis_index("col") % 2 == 0

    def own_row(ref, second_core_ref, q):
        return jnp.concatenate([ref[q, k] for k in range(slots)], axis=1)

    def pair_row(ref, second_core_ref, q):
        return jnp.concatenate([jnp.where(first_core, ref[q, k], second_core_ref[q, k]) for k in range(slots)], axis=1)

    sides = ((a_own, p_own, row, own_row), (a_or_p, p_or_a, row ^ 4, pair_row))
    fine = [(*side, q, (side[2] * nfiber + fiber) * rows + q) for side in sides for q in range(rows)]
    products = []
    for a_ref, p_ref, panel, blocks, q, i in fine:
        neighbours = []
        for k in range(slots):
            j = columns_ref[k, i]
            near_slot, far_slot = slot_of(j // 4, NEAR), later_slot(j // 4)
            near = (j // 2) % 2 == fiber
            place = pl.ds(pl.multiple_of(j % 2 * HALF, HALF), HALF)
            block, codes = [
                jnp.where(near, near_ref[near_slot, part].astype(jnp.int32), far_ref[far_slot, part].astype(jnp.int32))
                for part in (place, slice(BLK, BLK + SCALE_ROWS))
            ]
            codes = jnp.where(j % 2 == 0, codes[0:1], codes[SCALE_ROWS // 2 : SCALE_ROWS // 2 + 1])
            block = block.astype(F32) * scale_of(codes)
            high = block.astype(BF16)
            rest = (block - high.astype(F32)).astype(BF16)
            neighbours.append(jnp.concatenate([high, rest], axis=0))
        products.append(
            lax.dot_general(
                jnp.concatenate(neighbours, axis=1),
                blocks(a_ref, p_ref, q),
                (((1,), (1,)), ((), ())),
                preferred_element_type=F32,
            )
        )
    lifted = []
    for (a_ref, p_ref, panel, blocks, q, i), y in zip(fine, products):
        y = y[:HALF] + y[HALF:]
        high = y.astype(BF16)
        rest = (y - high.astype(F32)).astype(BF16)
        both = jnp.dot(jnp.concatenate([high, rest], axis=0), blocks(p_ref, a_ref, q), preferred_element_type=F32)
        lifted.append(both[:HALF] + both[HALF:])
    for (a_ref, p_ref, panel, blocks, q, i), part in zip(fine, lifted):
        for k in range(slots):
            group = aggregates_ref[columns_ref[k, i]]
            total[group] += part[:, k * BLK : (k + 1) * BLK]
    for coarse in range(total.shape[0]):
        steps, scale = code(total[coarse])
        slot = later_slot(coarse)
        out_ref[slot, 0:HALF, :] = steps.astype(jnp.int16)
        out_ref[slot, HALF : HALF + SCALE_ROWS, :] = jnp.concatenate([scale, scale], axis=0).astype(jnp.int16)


def sum_kernel(parts_ref, out_ref):
    halves = [jnp.zeros((HALF, BLK), F32), jnp.zeros((HALF, BLK), F32)]
    for source in range(parts_ref.shape[0]):
        h = (source // 4) % 2
        slot = later_slot(source)
        factor = scale_of(parts_ref[slot, HALF : HALF + SCALE_ROWS, :].astype(jnp.int32))
        halves[h] = halves[h] + parts_ref[slot, 0:HALF, :].astype(jnp.int32).astype(F32) * factor
    steps, scale = code(jnp.concatenate(halves, axis=0).T)
    out_ref[0:BLK, :] = steps.astype(jnp.int16)
    out_ref[BLK : BLK + SCALE_ROWS, :] = jnp.concatenate([scale, scale], axis=0).astype(jnp.int16)


def add_kernel(layers_ref, out_ref):
    total = jnp.zeros_like(out_ref)
    for layer in range(layers_ref.shape[0]):
        factor = scale_of(layers_ref[layer, BLK : BLK + SCALE_ROWS, :].astype(jnp.int32))
        total = total + layers_ref[layer, 0:BLK, :].astype(jnp.int32).astype(F32) * factor
    out_ref[...] = total


SMEM = pl.BlockSpec(memory_space=pltpu.SMEM)
VMEM = pl.BlockSpec(memory_space=pltpu.VMEM)


def local(a_blocks, p_terms, block_columns, aggregates):
    nrow = lax.axis_size("row")
    ncol = lax.axis_size("col")
    nfiber = lax.axis_size("fiber")
    pairs = [(r, r ^ 4) for r in range(nrow)]

    def along(step):
        moves = []
        for c in range(ncol):
            for f in range(nfiber):
                z = (f * (ncol // 2) + c // 2 + step) % ncol
                moves.append((c * nfiber + f, (z % (ncol // 2) * 2 + c % 2) * nfiber + z // (ncol // 2)))
        return moves

    across = [
        (c * nfiber + f, (c + ncol // 2) % ncol * nfiber + 1 - f) for c in range(ncol) for f in range(nfiber)
    ]

    later = [[(turned(k) ^ LATER[c % 2]) * ncol + c for k in range(nrow)] for c in range(ncol)]

    def orders(masks):
        return [[(k ^ masks[c % 2]) * ncol + c for k in range(nrow)] for c in range(ncol)]

    columns = block_columns.T
    packed_rows = BLK + SCALE_ROWS
    partner, own = pl.pallas_call(
        build_kernel,
        out_shape=(
            jax.ShapeDtypeStruct((2, packed_rows, BLK), jnp.int16),
            jax.ShapeDtypeStruct((nrow, packed_rows, BLK), jnp.int16),
        ),
        in_specs=[SMEM, SMEM, VMEM],
        out_specs=(VMEM, VMEM),
        name="build",
    )(columns, aggregates, p_terms)
    here = jnp.where(lax.axis_index("col") % 2 == 0, a_blocks, p_terms)
    from_pair = lax.ppermute(here, "row", pairs)
    crossed = lax.ppermute(partner, ("col", "fiber"), across)
    near = lax.all_to_all(own, ("row", "col"), 0, 0, axis_index_groups=orders(NEAR), tiled=True)
    spread = pl.pallas_call(
        spread_kernel,
        out_shape=jax.ShapeDtypeStruct((nrow, packed_rows, BLK), jnp.int16),
        in_specs=[VMEM],
        out_specs=VMEM,
        cost_estimate=pl.CostEstimate(flops=2**37, bytes_accessed=2**21, transcendentals=0),
        compiler_params=pltpu.CompilerParams(vmem_limit_bytes=4 * 1024 * 1024),
        name="spread",
    )(crossed)
    far = lax.all_to_all(spread, ("row", "col"), 0, 0, axis_index_groups=later, tiled=True)
    from_core = lax.ppermute(from_pair, "col", [(c, c ^ 1) for c in range(ncol)])
    parts = pl.pallas_call(
        main_kernel,
        out_shape=jax.ShapeDtypeStruct((nrow, HALF + SCALE_ROWS, BLK), jnp.int16),
        in_specs=[SMEM, SMEM] + [VMEM] * 6,
        out_specs=VMEM,
        scratch_shapes=[pltpu.VMEM((nrow, HALF, BLK), F32)],
        compiler_params=pltpu.CompilerParams(vmem_limit_bytes=16 * 1024 * 1024),
        name="main",
    )(columns, aggregates, near, far, a_blocks, p_terms, from_pair, from_core)
    received = lax.all_to_all(parts, ("row", "col"), 0, 0, axis_index_groups=later, tiled=True)
    tile = pl.pallas_call(
        sum_kernel,
        out_shape=jax.ShapeDtypeStruct((packed_rows, BLK), jnp.int16),
        in_specs=[VMEM],
        out_specs=VMEM,
        compiler_params=pltpu.CompilerParams(vmem_limit_bytes=4 * 1024 * 1024),
        name="sum",
    )(received)
    layers = lax.all_gather(tile, "fiber")
    return pl.pallas_call(
        add_kernel,
        out_shape=jax.ShapeDtypeStruct((BLK, BLK), F32),
        in_specs=[VMEM],
        out_specs=VMEM,
        compiler_params=pltpu.CompilerParams(vmem_limit_bytes=4 * 1024 * 1024),
        name="add",
    )(layers)


def solution(mesh):
    in_specs = (
        P(("row", "fiber"), None, None, None),
        P(("row", "fiber"), None, None, None),
        P(),
        P(),
    )
    out_specs = P("row", "col")
    return jax.shard_map(local, mesh=mesh, in_specs=in_specs, out_specs=out_specs, check_vma=False)
```
